512 devices in a mesh: ep: 128 (over x, z, core), dp: 4 (over y).
Axes of the slice: x: 4, y: 4, z: 16, core: 2. Of those that a mesh axis runs over, the one named last changes fastest.
Arguments:
- tokens: bfloat16 [2, 2048, 2048], P(None, 'ep', 'dp'), may hold values from -6 to 6
- route_ids: int32 [2, 2048, 8], P(None, 'ep'), may hold values from 0 to 127, all different within a row; in each aligned block of 16 rows (0 to 15, 16 to 31, ..., all dimensions but the last counted through in order) at most 2 rows name the same one
- gate_vals: float32 [2, 2048, 8], P(None, 'ep'), may hold values from 0.05 to 1
- replica_choice: int32 [2, 128, 128], P(None, 'ep'), may hold values from 0 to 1
- placement: int32 [128, 2], replicated, may hold values from 0 to 127, as said below
- gate_up: bfloat16 [128, 2, 2048, 1536], P('ep', None, None, 'dp'), may hold values from -0.125 to 0.125
- down_proj: bfloat16 [128, 2, 768, 2048], P('ep', None, None, 'dp'), may hold values from -0.21875 to 0.21875
- changed_expert: int32 [128, 32], P('ep'), may hold values from 0 to 127, as said below
- changed_block: int32 [128, 32], P('ep'), may hold values from 0 to 255, as said below
- delta_gate_up: bfloat16 [128, 32, 8, 1536], P('ep', None, None, 'dp'), may hold values from -0.5 to 0.5
- delta_down: bfloat16 [128, 32, 3, 2048], P('ep', None, None, 'dp'), may hold values from -0.875 to 0.875
Outputs:
- layer_out: bfloat16 [2, 2048, 2048], P(None, 'ep', 'dp')
The draws below stay inside these ranges and needn't reach their ends.
Inputs may be any that keep to these rules, and one draw needn't show every extreme that they name: `placement`: column 0 is a permutation of the experts (the primary replicas) and so is column 1 (the redundant ones); an expert's two replicas lie on different devices. `changed_expert`: the 32 experts listed by one learner are distinct. `changed_block`: each pair of an expert and a block number appears at most once among all learners' lists. `route_ids`: within the 16 tokens of one device at one step, no expert is named by more than 2 tokens.
All inputs are finite; a program needn't handle non-finite values.
Results may differ from the reference program's by a relative error of at most 0.0072.
Values may be sent and summed in bfloat16 or wider, within the bound.
No kernel may reach another device: no remote copies, remote signals or barrier semaphores. Data moves between devices by JAX's collectives and lax.ppermute only.
A program may use at most 128 MiB of HBM per device.

```python
import math
import jax
import jax.numpy as jnp
import numpy as np
from jax import lax

D = 2048
HID = 768
TOP = 8
NBLK = 256
STEPS = 2
ROWS = 16
EXPERTS = 128
CHANGED = 32
CAP = 2
BR = 8
BR2 = 3
HD = 192
TOKENS = 2048
N_EP = 128
N_DP = 4


def changed_pair(key):
    key_experts = jax.random.fold_in(key, 11)
    key_blocks = jax.random.fold_in(key, 12)

    def learner_experts(learner_key):
        return jax.random.permutation(learner_key, EXPERTS)[:CHANGED]

    def expert_orders(order_key):
        return jax.random.permutation(order_key, NBLK)
    experts = jax.vmap(learner_experts)(jax.random.split(key_experts, N_EP)).astype(jnp.int32)
    orders = jax.vmap(expert_orders)(jax.random.split(key_blocks, EXPERTS)).astype(jnp.int32)
    learners = jnp.broadcast_to(jnp.arange(N_EP, dtype=jnp.int32)[:, None], experts.shape)
    blocks = orders[experts, learners].astype(jnp.int32)
    return (experts, blocks)


def draw_changed_expert(key, part):
    return changed_pair(key)[0]


def draw_changed_block(key, part):
    return changed_pair(key)[1]


def draw_placement(key, part):
    key = jax.random.fold_in(key, 3)
    first_key, second_key = jax.random.split(key)
    primary = jax.random.permutation(first_key, N_EP).astype(jnp.int32)
    order = jax.random.permutation(second_key, N_EP).astype(jnp.int32)
    successor = jnp.zeros((N_EP,), jnp.int32).at[order].set(jnp.roll(order, -1))
    redundant = primary[successor]
    return jnp.stack([primary, redundant], axis=1).astype(jnp.int32)


def set_ends(result, rng, smallest, high):
    extent = result.shape
    spot = [jax.random.randint(jax.random.fold_in(rng, axis), (), 0, extent[axis]) for axis in range(len(extent))]
    result = result.at[tuple(spot)].set(smallest)
    longest = extent.index(max(extent))
    spot[longest] = (spot[longest] + 1) % extent[longest]
    return result.at[tuple(spot)].set(high)


def shard_levels(own_key, shape, cuts, smallest, largest):
    factor_of = 1.0
    for dim, shards_of in cuts:
        heights = jax.random.uniform(jax.random.fold_in(jax.random.fold_in(own_key, 6), dim), (shards_of,), jnp.float32, smallest / len(cuts), largest / len(cuts))
        factor_of = factor_of * jnp.repeat(jnp.exp(heights), shape[dim] // shards_of).reshape((-1,) + (1,) * (len(shape) - 1 - dim))
    return factor_of


def assign_block(rng, own, number, rows, count, top, reach, lean):
    order = jax.random.permutation(rng, count)
    crowded, common = load_shares(count, rows * top, reach, lean, True), load_shares(count, rows * top, reach, lean, False)
    places = jnp.arange(count)

    def named(tallies, turn):
        used = int((tallies > 0).sum())
        fixed = max(1, used // 4)
        passed = fixed + (places - fixed + turn * (used - fixed)) % max(1, count - fixed)
        return jnp.zeros((count,), jnp.int32).at[order[jnp.where(places < fixed, places, passed)]].set(jnp.asarray(tallies, jnp.int32))

    tallies = jnp.where(number % 4 == 0, named(crowded, number // 4), named(common, number - number // 4 - 1))
    mixed = jax.random.permutation(jax.random.fold_in(own, 3), count)
    source_of, receiver = mixed[0:count // 2 * 2:2], mixed[1:count // 2 * 2:2]
    margin = jnp.minimum(tallies[source_of] - 1, reach - tallies[receiver]) // 2
    margin = jnp.where((source_of == order[0]) | (receiver == order[0]) | (tallies[receiver] == 0), 0, jnp.maximum(margin, 0))
    passed = jax.random.randint(jax.random.fold_in(own, 4), (count // 2,), 0, 1 << 20) % (margin + 1)
    tallies = tallies.at[source_of].add(-passed).at[receiver].add(passed)
    items = jnp.searchsorted(jnp.cumsum(tallies), jnp.arange(rows * top), side="right").astype(jnp.int32)
    grid = items.reshape(top, rows).T
    grid = grid[jax.random.permutation(jax.random.fold_in(own, 1), rows)]
    turn = jax.random.randint(jax.random.fold_in(own, 2), (rows, 1), 0, top)
    return jnp.take_along_axis(grid, (jnp.arange(top)[None, :] + turn) % top, axis=1)


def load_shares(number_of, total, limit, slope, full):
    portions = [(1 << 20) // math.isqrt(standing ** slope) + 1 for standing in range(1, number_of + 1)]
    largest = limit if full else min(limit, max(-(-total // number_of), total * portions[0] // sum(portions)))
    least = 1 if total - largest >= number_of - 1 else 0
    holding, rest = [largest] + [least] * (number_of - 1), total - largest - least * (number_of - 1)
    while rest > 0:
        candidates = [i for i in range(1, number_of) if holding[i] < largest] or [i for i in range(1, number_of) if holding[i] < limit]
        pool, budget = sum([portions[i] for i in candidates]), rest
        for i in candidates:
            extra = min(limit - holding[i], max(1, budget * portions[i] // pool), rest)
            holding[i] = holding[i] + extra
            rest = rest - extra
    return np.array(holding)


def bell_draw(rng, extent, deviation, limit, cuts=(), kind=jnp.bfloat16):
    loudness = shard_levels(rng, extent, cuts, -0.22, 0.18) if cuts else 1.0
    entries = jax.random.normal(rng, extent, jnp.float32) * deviation * loudness
    return jnp.minimum(jnp.maximum(entries, -limit), limit).astype(kind)


def setup_inputs(seed: int = 0) -> dict:
    key_list = jax.random.split(jax.random.key(seed), 12)
    tokens = bell_draw(key_list[0], (STEPS, TOKENS, D), 1.0, 6.0, ((1, 128), (2, 4)))
    route_ids_keys = jax.random.split(jax.random.fold_in(key_list[1], 1), STEPS * TOKENS // ROWS)
    route_ids_turns = jax.random.permutation(jax.random.fold_in(key_list[1], 3), STEPS * TOKENS // ROWS)
    route_ids = jax.vmap(lambda own, number: assign_block(jax.random.fold_in(key_list[1], 2), own, number, ROWS, EXPERTS, TOP, CAP, 2))(route_ids_keys, route_ids_turns).reshape((STEPS, TOKENS, TOP))
    gate_vals = jnp.clip(jnp.exp(math.log(1.0) - 2.9957323 * jax.random.uniform(key_list[2], (STEPS, TOKENS, TOP), jnp.float32) ** shard_levels(key_list[2], (STEPS, TOKENS, TOP), ((1, 128),), -0.2, 0.2)), 0.05, 1.0)
    replica_choice = set_ends(jax.random.randint(key_list[3], (STEPS, N_EP, EXPERTS), 0, 2), jax.random.fold_in(key_list[3], 1), 0, 1).astype(jnp.int32)
    placement = draw_placement(jax.random.fold_in(key_list[11], 71), 0)
    gate_up = bell_draw(key_list[5], (N_EP, 2, D, 2 * HID), D ** -0.5, 0.125, ((0, 128), (3, 4)))
    down_proj = bell_draw(key_list[6], (N_EP, 2, HID, D), HID ** -0.5, 0.21875, ((0, 128), (3, 4)))
    changed_expert = draw_changed_expert(jax.random.fold_in(key_list[11], 71), 0)
    changed_block = draw_changed_block(jax.random.fold_in(key_list[11], 71), 0)
    delta_gate_up = bell_draw(key_list[9], (N_EP, CHANGED, BR, 2 * HID), (D // 16) ** -0.5, 0.5, ((0, 128), (3, 4)))
    delta_down = bell_draw(key_list[10], (N_EP, CHANGED, BR2, D), (HID // 16) ** -0.5, 0.875, ((0, 128), (3, 4)))
    return {"tokens": tokens, "route_ids": route_ids, "gate_vals": gate_vals, "replica_choice": replica_choice, "placement": placement, "gate_up": gate_up, "down_proj": down_proj, "changed_expert": changed_expert, "changed_block": changed_block, "delta_gate_up": delta_gate_up, "delta_down": delta_down}


def slot_targets(route_step, choice_step, host):
    expert_ids = jnp.arange(EXPERTS, dtype=jnp.int32)
    route_blocks = route_step.reshape(N_EP, ROWS * TOP)
    expert_hits = (route_blocks[:, :, None] == expert_ids[None, None, :]).astype(jnp.int32)
    before = jnp.cumsum(expert_hits, axis=1) - expert_hits
    position = jnp.sum(before * expert_hits, axis=2).astype(jnp.int32)
    source = jnp.broadcast_to(jnp.arange(N_EP, dtype=jnp.int32)[:, None], route_blocks.shape)
    replica = choice_step[source, route_blocks].astype(jnp.int32)
    device_to = host[route_blocks, replica].astype(jnp.int32)
    flat = ((device_to * 2 + replica) * N_EP + source) * CAP + position
    return flat.reshape(TOKENS, TOP).astype(jnp.int32)


def reference(tokens, route_ids, gate_vals, replica_choice, placement, gate_up, down_proj, changed_expert, changed_block, delta_gate_up, delta_down):
    expert_ids = jnp.arange(EXPERTS, dtype=jnp.int32)
    device_ids = jnp.arange(N_EP, dtype=jnp.int32)
    host = jnp.sum(device_ids[:, None, None] * (placement[:, None, :] == expert_ids[None, :, None]).astype(jnp.int32), axis=0).astype(jnp.int32)
    slot_rows = N_EP * CAP
    targets = []
    buffers = []
    for step_index in range(STEPS):
        flat = slot_targets(route_ids[step_index], replica_choice[step_index], host)
        targets.append(flat)
        copies = jnp.broadcast_to(tokens[step_index][:, None, :], (TOKENS, TOP, D)).reshape(TOKENS * TOP, D)
        buffer = jnp.zeros((N_EP * 2 * slot_rows, D), jnp.bfloat16).at[flat.reshape(-1)].set(copies)
        buffers.append(buffer)
    stacked = jnp.stack(buffers).reshape(STEPS, N_EP, 2, slot_rows, D).transpose(1, 2, 0, 3, 4)

    table = jnp.full((EXPERTS, NBLK), -1, jnp.int32)
    table = table.at[changed_expert.reshape(-1), changed_block.reshape(-1)].set(jnp.arange(N_EP * CHANGED, dtype=jnp.int32))
    gate_deltas = delta_gate_up.reshape(N_EP * CHANGED, BR * 2 * HID)
    down_deltas = delta_down.reshape(N_EP * CHANGED, BR2 * D)

    def serve_device(inputs):
        weights_gu, weights_dn, hosted, batch = inputs
        results = []
        for slot_index in range(2):
            source_rows = table[hosted[slot_index]]
            present = source_rows >= 0
            safe_rows = jnp.maximum(source_rows, 0)
            add_gu = jnp.where(present[:, None], gate_deltas[safe_rows], jnp.zeros((), jnp.bfloat16)).reshape(D, 2 * HID)
            add_dn = jnp.where(present[:, None], down_deltas[safe_rows], jnp.zeros((), jnp.bfloat16)).reshape(HID, D)
            fresh_gu = (weights_gu[slot_index].astype(jnp.float32) + add_gu.astype(jnp.float32)).astype(jnp.bfloat16)
            fresh_dn = (weights_dn[slot_index].astype(jnp.float32) + add_dn.astype(jnp.float32)).astype(jnp.bfloat16)
            ordered_gu = fresh_gu.reshape(D, N_DP, 2, HD).transpose(0, 2, 1, 3).reshape(D, 2 * HID)
            rows_in = batch[slot_index].reshape(STEPS * slot_rows, D)
            mixed = jnp.dot(rows_in, ordered_gu, preferred_element_type=jnp.float32).reshape(-1, 2, HID)
            hidden = (jax.nn.silu(mixed[:, 0]) * mixed[:, 1]).astype(jnp.bfloat16)
            output = jnp.dot(hidden, fresh_dn, preferred_element_type=jnp.float32).astype(jnp.bfloat16)
            results.append(output.reshape(STEPS, slot_rows, D))
        return jnp.stack(results)

    served = lax.map(serve_device, (gate_up, down_proj, placement, stacked))
    flat_served = served.transpose(2, 0, 1, 3, 4).reshape(STEPS, N_EP * 2 * slot_rows, D)
    outputs = []
    for step_index in range(STEPS):
        picked = flat_served[step_index][targets[step_index]].astype(jnp.float32)
        mixed_out = jnp.sum(gate_vals[step_index][:, :, None] * picked, axis=1)
        outputs.append(mixed_out.astype(jnp.bfloat16))
    return jnp.stack(outputs)
```

```python
import functools

import jax
import jax.numpy as jnp
from jax import lax
from jax.experimental import pallas as pl
from jax.experimental.pallas import tpu as pltpu
from jax.sharding import Mesh, PartitionSpec as P

NX = 4
NC = 2
EP = ("x", "z", "c")
XC = ("x", "c")
CAP = 2
META = 128
BF = jnp.bfloat16
F32 = jnp.float32
PARAMS = pltpu.CompilerParams(vmem_limit_bytes=40 * 1024 * 1024)


def slot_codes(route, choice, placement):
    steps, rows, top = route.shape
    experts = choice.shape[1]
    devices = placement.shape[0]
    expert_ids = jnp.arange(experts, dtype=jnp.int32)
    device_ids = jnp.arange(devices, dtype=jnp.int32)
    host = jnp.sum(
        jnp.where(placement[:, :, None] == expert_ids, device_ids[:, None, None], 0), axis=0
    )
    table = jnp.where(choice == 1, host[1] * 2 + 1, host[0] * 2)
    flat = route.reshape(steps, rows * top)
    slot = jnp.sum(
        jnp.where(flat[:, :, None] == expert_ids, table[:, None, :], 0), axis=2
    )
    order = jnp.arange(rows * top, dtype=jnp.int32)
    position = jnp.sum(
        ((flat[:, :, None] == flat[:, None, :]) & (order[None, :] < order[:, None])).astype(
            jnp.int32
        ),
        axis=2,
    )
    return (slot * CAP + position - devices * CAP).reshape(steps, rows, top)


def pick_kernel(tok_ref, code_ref, target_ref, label_ref, out_ref):
    zs, rows2, _ = tok_ref.shape
    peers, _, width = out_ref.shape
    steps, top, count = code_ref.shape
    rows = rows2 // steps
    slots = target_ref.shape[0]
    part = slots // (peers * 2)
    own = lax.broadcasted_iota(jnp.int32, (slots, count), 0) % part // CAP
    held = lax.broadcasted_iota(jnp.int32, (slots, count), 1) // rows
    same = own == held
    target = target_ref[...]
    for s in range(steps):
        hit = code_ref[s, 0:1, :] == target
        for k in range(1, top):
            hit = hit | (code_ref[s, k : k + 1, :] == target)
        pick = jnp.where(hit & same, 1.0, 0.0).astype(BF)
        toks = tok_ref[:, s * rows : (s + 1) * rows, :width].reshape(count, width)
        got = jnp.dot(pick, toks, preferred_element_type=F32).astype(BF)
        got = got.reshape(peers, 2, part, width)
        for j in range(2):
            start = (j * steps + s) * part
            out_ref[:, start : start + part, :] = got[:, j]
    out_ref[:, 2 * steps * part :, :] = label_ref[...]


def pick_rows(packets, codes_t, target_col, labels, width, peers, rows):
    return pl.pallas_call(
        pick_kernel,
        out_shape=jax.ShapeDtypeStruct((peers, rows + 16, width), BF),
        compiler_params=PARAMS,
        cost_estimate=pl.CostEstimate(
            flops=4 * codes_t.shape[2] * target_col.shape[0] * width,
            bytes_accessed=4 * 1024 * 1024,
            transcendentals=0,
        ),
    )(packets, codes_t, target_col, labels)


def gate_kernel(br, where_ref, w_ref, d_ref, t_ref, *refs):
    tok_refs, out_ref, cat_ref = refs[:-2], refs[-2], refs[-1]
    peers, zs, _ = d_ref.shape
    depth, cols = w_ref.shape[1:]
    learners = peers * zs
    quarter = tok_refs[0].shape[2]
    parts = len(tok_refs)
    for r in range(br):
        cat_ref[r * learners : (r + 1) * learners, :] = d_ref[
            :, :, r * cols : (r + 1) * cols
        ].reshape(learners, cols)
    chunk = min(256, quarter)
    row_ids = lax.broadcasted_iota(jnp.int32, (chunk, br * learners), 0)
    tgt = t_ref[0]
    acc = None
    for n in range(parts):
        q = where_ref[n]
        for c in range(quarter // chunk):
            base = pl.multiple_of(q * quarter + c * chunk, chunk)
            spread = jnp.where(row_ids == tgt - base, 1.0, 0.0).astype(BF)
            update = jnp.dot(spread, cat_ref[...], preferred_element_type=F32)
            fresh = (w_ref[0, pl.ds(base, chunk), :].astype(F32) + update).astype(BF)
            toks = tok_refs[n][:, :, c * chunk : (c + 1) * chunk].reshape(-1, chunk)
            term = jnp.dot(toks, fresh, preferred_element_type=F32)
            acc = term if acc is None else acc + term
    half = cols // 2
    up = pltpu.roll(acc, half, 1)
    act = acc / (1.0 + jnp.exp(-acc)) * up
    out_ref[0] = act[:, :half].astype(BF)


def gate_hidden(where, gate_up, deltas, targets, toks, br):
    _, depth, cols = gate_up.shape
    peers, rows, quarter = toks[0].shape
    zs = deltas.shape[1] // 2
    slot_rows = peers * rows // 2
    learners = peers * zs
    grid_spec = pltpu.PrefetchScalarGridSpec(
        num_scalar_prefetch=1,
        grid=(2,),
        in_specs=[
            pl.BlockSpec((1, depth, cols), lambda j, w: (j, 0, 0)),
            pl.BlockSpec((peers, zs, deltas.shape[2]), lambda j, w: (0, j, 0)),
            pl.BlockSpec((1, 1, br * learners), lambda j, w: (j, 0, 0)),
        ]
        + [pl.BlockSpec((peers, rows // 2, quarter), lambda j, w: (0, j, 0))] * len(toks),
        out_specs=pl.BlockSpec((1, slot_rows, cols // 2), lambda j, w: (j, 0, 0)),
        scratch_shapes=[pltpu.VMEM((br * learners, cols), BF)],
    )
    return pl.pallas_call(
        functools.partial(gate_kernel, br),
        grid_spec=grid_spec,
        out_shape=jax.ShapeDtypeStruct((2, slot_rows, cols // 2), BF),
        compiler_params=PARAMS,
        cost_estimate=pl.CostEstimate(
            flops=4 * depth * cols * (slot_rows + br * learners),
            bytes_accessed=10 * 1024 * 1024,
            transcendentals=2 * slot_rows * cols,
        ),
    )(where, gate_up, deltas, targets, *toks)


def down_kernel(br, w_ref, d_ref, t_ref, out_ref, cat_ref):
    peers, zs, _ = d_ref.shape
    depth, cols = w_ref.shape[1:]
    learners = peers * zs
    for r in range(br):
        cat_ref[r * learners : (r + 1) * learners, :] = d_ref[
            :, :, r * cols : (r + 1) * cols
        ].reshape(learners, cols)
    row_ids = lax.broadcasted_iota(jnp.int32, (depth, br * learners), 0)
    spread = jnp.where(row_ids == t_ref[0], 1.0, 0.0).astype(BF)
    update = jnp.dot(spread, cat_ref[...], preferred_element_type=F32)
    out_ref[0] = (w_ref[0].astype(F32) + update).astype(BF)


def fresh_down(down, deltas, targets, br):
    _, depth, cols = down.shape
    peers, zs = deltas.shape[0], deltas.shape[1] // 2
    learners = peers * zs
    return pl.pallas_call(
        functools.partial(down_kernel, br),
        grid=(2,),
        in_specs=[
            pl.BlockSpec((1, depth, cols), lambda j: (j, 0, 0)),
            pl.BlockSpec((peers, zs, deltas.shape[2]), lambda j: (0, j, 0)),
            pl.BlockSpec((1, 1, br * learners), lambda j: (j, 0, 0)),
        ],
        out_specs=pl.BlockSpec((1, depth, cols), lambda j: (j, 0, 0)),
        scratch_shapes=[pltpu.VMEM((br * learners, cols), BF)],
        out_shape=jax.ShapeDtypeStruct((2, depth, cols), BF),
        compiler_params=PARAMS,
        cost_estimate=pl.CostEstimate(
            flops=4 * depth * cols * br * learners,
            bytes_accessed=5 * 1024 * 1024,
            transcendentals=0,
        ),
    )(down, deltas, targets)


def out_kernel(peers, h0_ref, h1_ref, w_ref, out_ref):
    parts, slot_rows, hd = h0_ref.shape
    cols = w_ref.shape[2]
    for j, h_ref in enumerate((h0_ref, h1_ref)):
        acc = None
        for p in range(parts):
            term = jnp.dot(
                h_ref[p], w_ref[j, p * hd : (p + 1) * hd, :], preferred_element_type=F32
            )
            acc = term if acc is None else acc + term
        out_ref[:, j] = acc.astype(BF).reshape(peers, slot_rows // peers, cols)


def expert_out(h0, h1, down, peers):
    parts, slot_rows, hd = h0.shape
    cols = down.shape[2]
    return pl.pallas_call(
        functools.partial(out_kernel, peers),
        out_shape=jax.ShapeDtypeStruct((peers, 2, slot_rows // peers, cols), BF),
        compiler_params=PARAMS,
        cost_estimate=pl.CostEstimate(
            flops=4 * slot_rows * cols * parts * hd,
            bytes_accessed=5 * 1024 * 1024,
            transcendentals=0,
        ),
    )(h0, h1, down)


def mix_kernel(ret_ref, code_ref, gate_ref, target_ref, out_ref):
    peers, _, steps, part, width = ret_ref.shape
    _, count, top = code_ref.shape
    zs, rows2, _ = out_ref.shape
    rows = rows2 // steps
    slots = peers * 2 * part
    own = lax.broadcasted_iota(jnp.int32, (count, slots), 1) % part // CAP
    held = lax.broadcasted_iota(jnp.int32, (count, slots), 0) // rows
    same = own == held
    target = target_ref[...]
    for s in range(steps):
        weight = jnp.zeros((count, slots), F32)
        for k in range(top):
            hit = code_ref[s, :, k : k + 1] == target
            weight = jnp.where(hit, gate_ref[s, :, k : k + 1], weight)
        weight = jnp.where(same, weight, 0.0)
        back = ret_ref[:, :, s].reshape(slots, width)
        high = weight.astype(BF)
        rest = weight - high.astype(F32)
        mid = rest.astype(BF)
        low = (rest - mid.astype(F32)).astype(BF)
        total = (
            jnp.dot(high, back, preferred_element_type=F32)
            + jnp.dot(mid, back, preferred_element_type=F32)
            + jnp.dot(low, back, preferred_element_type=F32)
        )
        out_ref[:, s * rows : (s + 1) * rows, :] = total.astype(BF).reshape(zs, rows, width)


def mix_rows(back, codes, gates, target_row, zs, rows2):
    width = back.shape[-1]
    return pl.pallas_call(
        mix_kernel,
        out_shape=jax.ShapeDtypeStruct((zs, rows2, width), BF),
        compiler_params=PARAMS,
        cost_estimate=pl.CostEstimate(
            flops=12 * codes.shape[1] * target_row.shape[1] * width,
            bytes_accessed=2 * 1024 * 1024,
            transcendentals=0,
        ),
    )(back, codes, gates, target_row)


def on_device(
    tokens,
    route_ids,
    gate_vals,
    replica_choice,
    placement,
    gate_up,
    down_proj,
    changed_expert,
    changed_block,
    delta_gate_up,
    delta_down,
):
    nx, nz, nc, nd = (lax.axis_size(a) for a in ("x", "z", "c", "dp"))
    peers = nx * nc
    steps, rows, quarter = tokens.shape
    top = route_ids.shape[2]
    changed, br, gate_cols = delta_gate_up.shape[1:]
    br2, down_cols = delta_down.shape[2:]
    z = lax.axis_index("z")
    p = lax.axis_index("dp")

    flat_deltas = jnp.concatenate(
        [delta_gate_up.reshape(changed, -1), delta_down.reshape(changed, -1)], axis=1
    )
    deltas = lax.all_gather(flat_deltas, "z", axis=0, tiled=True)

    codes = slot_codes(route_ids, replica_choice[:, 0], placement)
    high = lax.reduce_precision(gate_vals, 8, 7)
    mid = lax.reduce_precision(gate_vals - high, 8, 7)
    low = gate_vals - high - mid
    meta = jnp.concatenate([codes.astype(F32), high, mid, low], axis=2).reshape(
        steps * rows, 4 * top
    )
    names = jnp.stack([changed_expert[0], changed_block[0]], axis=1).astype(F32)
    meta = jnp.concatenate([meta, names], axis=1)
    meta = jnp.pad(meta, ((0, 0), (0, META - meta.shape[1]))).astype(BF)
    packet = jnp.concatenate([tokens.reshape(steps * rows, quarter), meta], axis=1)
    packets = lax.all_gather(packet, "z", axis=0, tiled=False)

    metas = packets[:, :, quarter:].astype(F32)
    gathered = metas.reshape(nz, steps, rows, META).transpose(1, 0, 2, 3)
    gathered = gathered.reshape(steps, nz * rows, META)
    codes_all = gathered[:, :, :top]
    gates_all = (
        gathered[:, :, top : 2 * top]
        + gathered[:, :, 2 * top : 3 * top]
        + gathered[:, :, 3 * top : 4 * top]
    )
    codes_t = codes_all.transpose(0, 2, 1)
    names_expert = metas[:, :, 4 * top]
    names_block = metas[:, :, 4 * top + 1]

    devs = (
        jnp.arange(nx, dtype=jnp.int32)[:, None] * nz + z
    ) * nc + jnp.arange(nc, dtype=jnp.int32)[None, :]
    devs = devs.reshape(peers)
    slot_ids = devs[:, None] * 2 + jnp.arange(2, dtype=jnp.int32)[None, :]
    target = slot_ids[:, :, None, None] * CAP + jnp.arange(CAP, dtype=jnp.int32)
    target = jnp.broadcast_to(target, (peers, 2, nz, CAP)).reshape(-1)
    target = (target - nx * nz * nc * CAP).astype(F32)

    held = lax.dynamic_index_in_dim(
        placement.reshape(nx, nz, nc, 2), z, axis=1, keepdims=False
    ).reshape(peers, 2)
    held = held.astype(F32)
    match = held[:, :, None, None] == names_expert[None, None]
    labels = jnp.sum(jnp.where(match, names_block + 1.0, 0.0), axis=3)
    labels = labels.reshape(peers, 1, 2 * nz).astype(BF)
    labels = jnp.pad(labels, ((0, 0), (0, 15), (0, quarter - 2 * nz)))
    z_ids = jnp.arange(nz, dtype=jnp.int32)
    chosen = (
        match[:, :, None, :, :] & (z_ids[:, None] == z_ids[None, :])[None, None, :, :, None]
    )
    chosen = chosen.astype(BF).reshape(peers * 2 * nz, nz * changed)

    count_rows = 2 * steps * nz * CAP
    picked = pick_rows(
        packets, codes_t, target[:, None], labels, quarter, peers, count_rows
    )
    got = lax.all_to_all(picked, XC, split_axis=0, concat_axis=0, tiled=True)
    own = got[:, :count_rows]
    toks = [own] + [
        lax.ppermute(own, "dp", [(i, (i + n) % nd) for i in range(nd)]) for n in range(1, nd)
    ]
    where = jnp.stack([(p - n) % nd for n in range(nd)]).astype(jnp.int32)
    block_of = got[:, count_rows, : 2 * nz].astype(F32).astype(jnp.int32) - 1
    block_of = block_of.reshape(peers, 2, nz).transpose(1, 0, 2).reshape(2, 1, peers * nz)
    gate_targets = (block_of * br + jnp.arange(br, dtype=jnp.int32)[None, :, None]).reshape(
        2, 1, -1
    )
    down_targets = (block_of * br2 + jnp.arange(br2, dtype=jnp.int32)[None, :, None]).reshape(
        2, 1, -1
    )

    cut = br * gate_cols
    deltas, _ = lax.optimization_barrier((deltas, own))
    send_gate = jnp.dot(chosen, deltas[:, :cut], preferred_element_type=F32).astype(BF)
    got_gate = lax.all_to_all(
        send_gate.reshape(peers, 2 * nz, cut), XC, split_axis=0, concat_axis=0, tiled=True
    )
    got_gate, deltas = lax.optimization_barrier((got_gate, deltas))
    send_down = jnp.dot(chosen, deltas[:, cut:], preferred_element_type=F32).astype(BF)
    got_down = lax.all_to_all(
        send_down.reshape(peers, 2 * nz, br2 * down_cols),
        XC,
        split_axis=0,
        concat_axis=0,
        tiled=True,
    )

    hidden = gate_hidden(where, gate_up[0], got_gate, gate_targets, toks, br)
    down = fresh_down(down_proj[0], got_down, down_targets, br2)
    h0 = lax.all_gather(hidden[0], "dp", axis=0, tiled=False)
    h1 = lax.all_gather(hidden[1], "dp", axis=0, tiled=False)
    out = expert_out(h0, h1, down, peers).reshape(peers, count_rows, down_cols)

    back = lax.all_to_all(out, XC, split_axis=0, concat_axis=0, tiled=True)
    back = back.reshape(peers, 2, steps, nz * CAP, down_cols)
    partial = mix_rows(back, codes_all, gates_all, target[None, :], nz, steps * rows)
    final = lax.all_to_all(partial, "z", split_axis=0, concat_axis=0, tiled=True)
    total = jnp.sum(final.astype(F32), axis=0).astype(BF)
    return total.reshape(steps, rows, down_cols)


def solution(mesh):
    ep, nd = mesh.devices.shape
    cube = Mesh(mesh.devices.reshape(NX, ep // (NX * NC), NC, nd), EP + ("dp",))
    return jax.shard_map(
        on_device,
        mesh=cube,
        in_specs=(
            P(None, EP, "dp"),
            P(None, EP, None),
            P(None, EP, None),
            P(None, EP, None),
            P(),
            P(EP, None, None, "dp"),
            P(EP, None, None, "dp"),
            P(EP, None),
            P(EP, None),
            P(EP, None, None, "dp"),
            P(EP, None, None, "dp"),
        ),
        out_specs=P(None, EP, "dp"),
        check_vma=False,
    )
```

```python
import functools

import jax
import jax.numpy as jnp
from jax import lax
from jax.experimental import pallas as pl
from jax.experimental.pallas import tpu as pltpu
from jax.sharding import Mesh, PartitionSpec as P

NX = 4
NC = 2
EP = ("x", "z", "c")
XC = ("x", "c")
CAP = 2
META = 128
BF = jnp.bfloat16
F32 = jnp.float32
PARAMS = pltpu.CompilerParams(vmem_limit_bytes=40 * 1024 * 1024)


def slot_codes(route, choice, placement):
    steps, rows, top = route.shape
    experts = choice.shape[1]
    devices = placement.shape[0]
    expert_ids = jnp.arange(experts, dtype=jnp.int32)
    device_ids = jnp.arange(devices, dtype=jnp.int32)
    host = jnp.sum(
        jnp.where(placement[:, :, None] == expert_ids, device_ids[:, None, None], 0), axis=0
    )
    table = jnp.where(choice == 1, host[1] * 2 + 1, host[0] * 2)
    flat = route.reshape(steps, rows * top)
    slot = jnp.sum(
        jnp.where(flat[:, :, None] == expert_ids, table[:, None, :], 0), axis=2
    )
    order = jnp.arange(rows * top, dtype=jnp.int32)
    position = jnp.sum(
        ((flat[:, :, None] == flat[:, None, :]) & (order[None, :] < order[:, None])).astype(
            jnp.int32
        ),
        axis=2,
    )
    return (slot * CAP + position - devices * CAP).reshape(steps, rows, top)


def pick_kernel(tok_ref, code_ref, target_ref, label_ref, out_ref):
    zs, rows2, _ = tok_ref.shape
    peers, _, width = out_ref.shape
    steps, top, count = code_ref.shape
    rows = rows2 // steps
    slots = target_ref.shape[0]
    part = slots // (peers * 2)
    own = lax.broadcasted_iota(jnp.int32, (slots, count), 0) % part // CAP
    held = lax.broadcasted_iota(jnp.int32, (slots, count), 1) // rows
    same = own == held
    target = target_ref[...]
    for s in range(steps):
        hit = code_ref[s, 0:1, :] == target
        for k in range(1, top):
            hit = hit | (code_ref[s, k : k + 1, :] == target)
        pick = jnp.where(hit & same, 1.0, 0.0).astype(BF)
        toks = tok_ref[:, s * rows : (s + 1) * rows, :width].reshape(count, width)
        got = jnp.dot(pick, toks, preferred_element_type=F32).astype(BF)
        got = got.reshape(peers, 2, part, width)
        for j in range(2):
            start = (j * steps + s) * part
            out_ref[:, start : start + part, :] = got[:, j]
    out_ref[:, 2 * steps * part :, :] = label_ref[...]


def pick_rows(packets, codes_t, target_col, labels, width, peers, rows):
    return pl.pallas_call(
        pick_kernel,
        out_shape=jax.ShapeDtypeStruct((peers, rows + 16, width), BF),
        compiler_params=PARAMS,
        cost_estimate=pl.CostEstimate(
            flops=4 * codes_t.shape[2] * target_col.shape[0] * width,
            bytes_accessed=4 * 1024 * 1024,
            transcendentals=0,
        ),
    )(packets, codes_t, target_col, labels)


def gate_kernel(br, where_ref, w_ref, d_ref, t_ref, *refs):
    tok_refs, out_ref, cat_ref = refs[:-2], refs[-2], refs[-1]
    peers, zs, _ = d_ref.shape
    depth, cols = w_ref.shape[1:]
    learners = peers * zs
    quarter = tok_refs[0].shape[2]
    parts = len(tok_refs)
    for r in range(br):
        cat_ref[r * learners : (r + 1) * learners, :] = d_ref[
            :, :, r * cols : (r + 1) * cols
        ].reshape(learners, cols)
    chunk = min(256, quarter)
    row_ids = lax.broadcasted_iota(jnp.int32, (chunk, br * learners), 0)
    tgt = t_ref[0]
    acc = None
    for n in range(parts):
        q = where_ref[n]
        for c in range(quarter // chunk):
            base = pl.multiple_of(q * quarter + c * chunk, chunk)
            spread = jnp.where(row_ids == tgt - base, 1.0, 0.0).astype(BF)
            update = jnp.dot(spread, cat_ref[...], preferred_element_type=F32)
            fresh = (w_ref[0, pl.ds(base, chunk), :].astype(F32) + update).astype(BF)
            toks = tok_refs[n][:, :, c * chunk : (c + 1) * chunk].reshape(-1, chunk)
            term = jnp.dot(toks, fresh, preferred_element_type=F32)
            acc = term if acc is None else acc + term
    half = cols // 2
    up = pltpu.roll(acc, half, 1)
    act = acc / (1.0 + jnp.exp(-acc)) * up
    out_ref[0] = act.T[:half].astype(BF)


def gate_hidden(where, gate_up, deltas, targets, toks, br):
    _, depth, cols = gate_up.shape
    peers, rows, quarter = toks[0].shape
    zs = deltas.shape[1] // 2
    slot_rows = peers * rows // 2
    learners = peers * zs
    grid_spec = pltpu.PrefetchScalarGridSpec(
        num_scalar_prefetch=1,
        grid=(2,),
        in_specs=[
            pl.BlockSpec((1, depth, cols), lambda j, w: (j, 0, 0)),
            pl.BlockSpec((peers, zs, deltas.shape[2]), lambda j, w: (0, j, 0)),
            pl.BlockSpec((1, 1, br * learners), lambda j, w: (j, 0, 0)),
        ]
        + [pl.BlockSpec((peers, rows // 2, quarter), lambda j, w: (0, j, 0))] * len(toks),
        out_specs=pl.BlockSpec((1, cols // 2, slot_rows), lambda j, w: (j, 0, 0)),
        scratch_shapes=[pltpu.VMEM((br * learners, cols), BF)],
    )
    return pl.pallas_call(
        functools.partial(gate_kernel, br),
        grid_spec=grid_spec,
        out_shape=jax.ShapeDtypeStruct((2, cols // 2, slot_rows), BF),
        compiler_params=PARAMS,
        cost_estimate=pl.CostEstimate(
            flops=4 * depth * cols * (slot_rows + br * learners),
            bytes_accessed=10 * 1024 * 1024,
            transcendentals=2 * slot_rows * cols,
        ),
    )(where, gate_up, deltas, targets, *toks)


def down_kernel(br, w_ref, d_ref, t_ref, out_ref, cat_ref):
    peers, zs, _ = d_ref.shape
    depth, cols = w_ref.shape[1:]
    learners = peers * zs
    for r in range(br):
        cat_ref[r * learners : (r + 1) * learners, :] = d_ref[
            :, :, r * cols : (r + 1) * cols
        ].reshape(learners, cols)
    row_ids = lax.broadcasted_iota(jnp.int32, (depth, br * learners), 0)
    spread = jnp.where(row_ids == t_ref[0], 1.0, 0.0).astype(BF)
    update = jnp.dot(spread, cat_ref[...], preferred_element_type=F32)
    out_ref[0] = (w_ref[0].astype(F32) + update).astype(BF)


def fresh_down(down, deltas, targets, br):
    _, depth, cols = down.shape
    peers, zs = deltas.shape[0], deltas.shape[1] // 2
    learners = peers * zs
    return pl.pallas_call(
        functools.partial(down_kernel, br),
        grid=(2,),
        in_specs=[
            pl.BlockSpec((1, depth, cols), lambda j: (j, 0, 0)),
            pl.BlockSpec((peers, zs, deltas.shape[2]), lambda j: (0, j, 0)),
            pl.BlockSpec((1, 1, br * learners), lambda j: (j, 0, 0)),
        ],
        out_specs=pl.BlockSpec((1, depth, cols), lambda j: (j, 0, 0)),
        scratch_shapes=[pltpu.VMEM((br * learners, cols), BF)],
        out_shape=jax.ShapeDtypeStruct((2, depth, cols), BF),
        compiler_params=PARAMS,
        cost_estimate=pl.CostEstimate(
            flops=4 * depth * cols * br * learners,
            bytes_accessed=5 * 1024 * 1024,
            transcendentals=0,
        ),
    )(down, deltas, targets)


def out_kernel(peers, h0_ref, h1_ref, w_ref, out_ref):
    parts, hd, slot_rows = h0_ref.shape
    cols = w_ref.shape[2]
    for j, h_ref in enumerate((h0_ref, h1_ref)):
        acc = None
        for p in range(parts):
            term = lax.dot_general(
                h_ref[p],
                w_ref[j, p * hd : (p + 1) * hd, :],
                (((0,), (0,)), ((), ())),
                preferred_element_type=F32,
            )
            acc = term if acc is None else acc + term
        out_ref[:, j] = acc.astype(BF).reshape(peers, slot_rows // peers, cols)


def expert_out(h0, h1, down, peers):
    parts, hd, slot_rows = h0.shape
    cols = down.shape[2]
    return pl.pallas_call(
        functools.partial(out_kernel, peers),
        out_shape=jax.ShapeDtypeStruct((peers, 2, slot_rows // peers, cols), BF),
        compiler_params=PARAMS,
        cost_estimate=pl.CostEstimate(
            flops=4 * slot_rows * cols * parts * hd,
            bytes_accessed=5 * 1024 * 1024,
            transcendentals=0,
        ),
    )(h0, h1, down)


def mix_kernel(ret_ref, code_ref, gate_ref, target_ref, out_ref):
    peers, _, steps, part, width = ret_ref.shape
    _, count, top = code_ref.shape
    zs, rows2, _ = out_ref.shape
    rows = rows2 // steps
    slots = peers * 2 * part
    own = lax.broadcasted_iota(jnp.int32, (count, slots), 1) % part // CAP
    held = lax.broadcasted_iota(jnp.int32, (count, slots), 0) // rows
    same = own == held
    target = target_ref[...]
    for s in range(steps):
        weight = jnp.zeros((count, slots), F32)
        for k in range(top):
            hit = code_ref[s, :, k : k + 1] == target
            weight = jnp.where(hit, gate_ref[s, :, k : k + 1], weight)
        weight = jnp.where(same, weight, 0.0)
        back = ret_ref[:, :, s].reshape(slots, width)
        high = weight.astype(BF)
        rest = weight - high.astype(F32)
        mid = rest.astype(BF)
        low = (rest - mid.astype(F32)).astype(BF)
        total = (
            jnp.dot(high, back, preferred_element_type=F32)
            + jnp.dot(mid, back, preferred_element_type=F32)
            + jnp.dot(low, back, preferred_element_type=F32)
        )
        out_ref[:, s * rows : (s + 1) * rows, :] = total.astype(BF).reshape(zs, rows, width)


def mix_rows(back, codes, gates, target_row, zs, rows2):
    width = back.shape[-1]
    return pl.pallas_call(
        mix_kernel,
        out_shape=jax.ShapeDtypeStruct((zs, rows2, width), BF),
        compiler_params=PARAMS,
        cost_estimate=pl.CostEstimate(
            flops=12 * codes.shape[1] * target_row.shape[1] * width,
            bytes_accessed=2 * 1024 * 1024,
            transcendentals=0,
        ),
    )(back, codes, gates, target_row)


def on_device(
    tokens,
    route_ids,
    gate_vals,
    replica_choice,
    placement,
    gate_up,
    down_proj,
    changed_expert,
    changed_block,
    delta_gate_up,
    delta_down,
):
    nx, nz, nc, nd = (lax.axis_size(a) for a in ("x", "z", "c", "dp"))
    peers = nx * nc
    steps, rows, quarter = tokens.shape
    top = route_ids.shape[2]
    changed, br, gate_cols = delta_gate_up.shape[1:]
    br2, down_cols = delta_down.shape[2:]
    z = lax.axis_index("z")
    p = lax.axis_index("dp")

    flat_deltas = jnp.concatenate(
        [delta_gate_up.reshape(changed, -1), delta_down.reshape(changed, -1)], axis=1
    )
    deltas = lax.all_gather(flat_deltas, "z", axis=0, tiled=True)

    codes = slot_codes(route_ids, replica_choice[:, 0], placement)
    high = lax.reduce_precision(gate_vals, 8, 7)
    mid = lax.reduce_precision(gate_vals - high, 8, 7)
    low = gate_vals - high - mid
    meta = jnp.concatenate([codes.astype(F32), high, mid, low], axis=2).reshape(
        steps * rows, 4 * top
    )
    names = jnp.stack([changed_expert[0], changed_block[0]], axis=1).astype(F32)
    meta = jnp.concatenate([meta, names], axis=1)
    meta = jnp.pad(meta, ((0, 0), (0, META - meta.shape[1]))).astype(BF)
    packet = jnp.concatenate([tokens.reshape(steps * rows, quarter), meta], axis=1)
    packets = lax.all_gather(packet, "z", axis=0, tiled=False)

    metas = packets[:, :, quarter:].astype(F32)
    gathered = metas.reshape(nz, steps, rows, META).transpose(1, 0, 2, 3)
    gathered = gathered.reshape(steps, nz * rows, META)
    codes_all = gathered[:, :, :top]
    gates_all = (
        gathered[:, :, top : 2 * top]
        + gathered[:, :, 2 * top : 3 * top]
        + gathered[:, :, 3 * top : 4 * top]
    )
    codes_t = codes_all.transpose(0, 2, 1)
    names_expert = metas[:, :, 4 * top]
    names_block = metas[:, :, 4 * top + 1]

    devs = (
        jnp.arange(nx, dtype=jnp.int32)[:, None] * nz + z
    ) * nc + jnp.arange(nc, dtype=jnp.int32)[None, :]
    devs = devs.reshape(peers)
    slot_ids = devs[:, None] * 2 + jnp.arange(2, dtype=jnp.int32)[None, :]
    target = slot_ids[:, :, None, None] * CAP + jnp.arange(CAP, dtype=jnp.int32)
    target = jnp.broadcast_to(target, (peers, 2, nz, CAP)).reshape(-1)
    target = (target - nx * nz * nc * CAP).astype(F32)

    held = lax.dynamic_index_in_dim(
        placement.reshape(nx, nz, nc, 2), z, axis=1, keepdims=False
    ).reshape(peers, 2)
    held = held.astype(F32)
    match = held[:, :, None, None] == names_expert[None, None]
    labels = jnp.sum(jnp.where(match, names_block + 1.0, 0.0), axis=3)
    labels = labels.reshape(peers, 1, 2 * nz).astype(BF)
    labels = jnp.pad(labels, ((0, 0), (0, 15), (0, quarter - 2 * nz)))
    z_ids = jnp.arange(nz, dtype=jnp.int32)
    chosen = (
        match[:, :, None, :, :] & (z_ids[:, None] == z_ids[None, :])[None, None, :, :, None]
    )
    chosen = chosen.astype(BF).reshape(peers * 2 * nz, nz * changed)

    count_rows = 2 * steps * nz * CAP
    picked = pick_rows(
        packets, codes_t, target[:, None], labels, quarter, peers, count_rows
    )
    got = lax.all_to_all(picked, XC, split_axis=0, concat_axis=0, tiled=True)
    own = got[:, :count_rows]
    toks = [own] + [
        lax.ppermute(own, "dp", [(i, (i + n) % nd) for i in range(nd)]) for n in range(1, nd)
    ]
    where = jnp.stack([(p - n) % nd for n in range(nd)]).astype(jnp.int32)
    block_of = got[:, count_rows, : 2 * nz].astype(F32).astype(jnp.int32) - 1
    block_of = block_of.reshape(peers, 2, nz).transpose(1, 0, 2).reshape(2, 1, peers * nz)
    gate_targets = (block_of * br + jnp.arange(br, dtype=jnp.int32)[None, :, None]).reshape(
        2, 1, -1
    )
    down_targets = (block_of * br2 + jnp.arange(br2, dtype=jnp.int32)[None, :, None]).reshape(
        2, 1, -1
    )

    cut = br * gate_cols
    deltas, *_ = lax.optimization_barrier((deltas, toks[1], toks[-1]))
    send_gate = jnp.dot(chosen, deltas[:, :cut], preferred_element_type=F32).astype(BF)
    got_gate = lax.all_to_all(
        send_gate.reshape(peers, 2 * nz, cut), XC, split_axis=0, concat_axis=0, tiled=True
    )
    got_gate, deltas = lax.optimization_barrier((got_gate, deltas))
    send_down = jnp.dot(chosen, deltas[:, cut:], preferred_element_type=F32).astype(BF)
    got_down = lax.all_to_all(
        send_down.reshape(peers, 2 * nz, br2 * down_cols),
        XC,
        split_axis=0,
        concat_axis=0,
        tiled=True,
    )

    hidden = gate_hidden(where, gate_up[0], got_gate, gate_targets, toks, br)
    down = fresh_down(down_proj[0], got_down, down_targets, br2)
    h0 = lax.all_gather(hidden[0], "dp", axis=0, tiled=False)
    h1 = lax.all_gather(hidden[1], "dp", axis=0, tiled=False)
    out = expert_out(h0, h1, down, peers).reshape(peers, count_rows, down_cols)

    back = lax.all_to_all(out, XC, split_axis=0, concat_axis=0, tiled=True)
    back = back.reshape(peers, 2, steps, nz * CAP, down_cols)
    partial = mix_rows(back, codes_all, gates_all, target[None, :], nz, steps * rows)
    final = lax.all_to_all(partial, "z", split_axis=0, concat_axis=0, tiled=True)
    total = jnp.sum(final.astype(F32), axis=0).astype(BF)
    return total.reshape(steps, rows, down_cols)


def solution(mesh):
    ep, nd = mesh.devices.shape
    cube = Mesh(mesh.devices.reshape(NX, ep // (NX * NC), NC, nd), EP + ("dp",))
    return jax.shard_map(
        on_device,
        mesh=cube,
        in_specs=(
            P(None, EP, "dp"),
            P(None, EP, None),
            P(None, EP, None),
            P(None, EP, None),
            P(),
            P(EP, None, None, "dp"),
            P(EP, None, None, "dp"),
            P(EP, None),
            P(EP, None),
            P(EP, None, None, "dp"),
            P(EP, None, None, "dp"),
        ),
        out_specs=P(None, EP, "dp"),
        check_vma=False,
    )
```

```python
import functools

import jax
import jax.numpy as jnp
from jax import lax
from jax.experimental import pallas as pl
from jax.experimental.pallas import tpu as pltpu
from jax.sharding import Mesh, PartitionSpec as P

NX = 4
NC = 2
EP = ("x", "z", "c")
XC = ("x", "c")
CAP = 2
META = 128
BF = jnp.bfloat16
F32 = jnp.float32
PARAMS = pltpu.CompilerParams(vmem_limit_bytes=40 * 1024 * 1024)


def slot_codes(route, choice, placement):
    steps, rows, top = route.shape
    experts = choice.shape[1]
    devices = placement.shape[0]
    expert_ids = jnp.arange(experts, dtype=jnp.int32)
    device_ids = jnp.arange(devices, dtype=jnp.int32)
    host = jnp.sum(
        jnp.where(placement[:, :, None] == expert_ids, device_ids[:, None, None], 0), axis=0
    )
    table = jnp.where(choice == 1, host[1] * 2 + 1, host[0] * 2)
    flat = route.reshape(steps, rows * top)
    slot = jnp.sum(
        jnp.where(flat[:, :, None] == expert_ids, table[:, None, :], 0), axis=2
    )
    order = jnp.arange(rows * top, dtype=jnp.int32)
    position = jnp.sum(
        ((flat[:, :, None] == flat[:, None, :]) & (order[None, :] < order[:, None])).astype(
            jnp.int32
        ),
        axis=2,
    )
    return (slot * CAP + position - devices * CAP).reshape(steps, rows, top)


def pick_kernel(tok_ref, code_ref, target_ref, label_ref, out_ref):
    zs, rows2, _ = tok_ref.shape
    peers, _, width = out_ref.shape
    steps, top, count = code_ref.shape
    rows = rows2 // steps
    slots = target_ref.shape[0]
    part = slots // (peers * 2)
    own = lax.broadcasted_iota(jnp.int32, (slots, count), 0) % part // CAP
    held = lax.broadcasted_iota(jnp.int32, (slots, count), 1) // rows
    same = own == held
    target = target_ref[...]
    for s in range(steps):
        hit = code_ref[s, 0:1, :] == target
        for k in range(1, top):
            hit = hit | (code_ref[s, k : k + 1, :] == target)
        pick = jnp.where(hit & same, 1.0, 0.0).astype(BF)
        toks = tok_ref[:, s * rows : (s + 1) * rows, :width].reshape(count, width)
        got = jnp.dot(pick, toks, preferred_element_type=F32).astype(BF)
        got = got.reshape(peers, 2, part, width)
        for j in range(2):
            start = (j * steps + s) * part
            out_ref[:, start : start + part, :] = got[:, j]
    out_ref[:, 2 * steps * part :, :] = label_ref[...]


def pick_rows(packets, codes_t, target_col, labels, width, peers, rows):
    return pl.pallas_call(
        pick_kernel,
        out_shape=jax.ShapeDtypeStruct((peers, rows + 16, width), BF),
        compiler_params=PARAMS,
        cost_estimate=pl.CostEstimate(
            flops=4 * codes_t.shape[2] * target_col.shape[0] * width,
            bytes_accessed=4 * 1024 * 1024,
            transcendentals=0,
        ),
    )(packets, codes_t, target_col, labels)


def gate_kernel(br, last, where_ref, w_ref, d_ref, t_ref, *refs):
    tok_refs, out_ref, cat_ref = refs[:-2], refs[-2], refs[-1]
    if last:
        tok_refs, sum_ref = tok_refs[:-1], tok_refs[-1]
    peers, zs, _ = d_ref.shape
    depth, cols = w_ref.shape[1:]
    learners = peers * zs
    quarter = tok_refs[0].shape[2]
    parts = len(tok_refs)
    for r in range(br):
        cat_ref[r * learners : (r + 1) * learners, :] = d_ref[
            :, :, r * cols : (r + 1) * cols
        ].reshape(learners, cols)
    chunk = min(256, quarter)
    row_ids = lax.broadcasted_iota(jnp.int32, (chunk, br * learners), 0)
    tgt = t_ref[0]
    acc = sum_ref[0] if last else None
    for n in range(parts):
        q = where_ref[n]
        for c in range(quarter // chunk):
            base = pl.multiple_of(q * quarter + c * chunk, chunk)
            spread = jnp.where(row_ids == tgt - base, 1.0, 0.0).astype(BF)
            update = jnp.dot(spread, cat_ref[...], preferred_element_type=F32)
            fresh = (w_ref[0, pl.ds(base, chunk), :].astype(F32) + update).astype(BF)
            toks = tok_refs[n][:, :, c * chunk : (c + 1) * chunk].reshape(-1, chunk)
            term = jnp.dot(toks, fresh, preferred_element_type=F32)
            acc = term if acc is None else acc + term
    if not last:
        out_ref[0] = acc
        return
    half = cols // 2
    up = pltpu.roll(acc, half, 1)
    act = acc / (1.0 + jnp.exp(-acc)) * up
    out_ref[0] = act.T[:half].astype(BF)


def gate_hidden(where, gate_up, deltas, targets, toks, br, sums=None):
    last = sums is not None
    _, depth, cols = gate_up.shape
    peers, rows, quarter = toks[0].shape
    zs = deltas.shape[1] // 2
    slot_rows = peers * rows // 2
    learners = peers * zs
    shape = (cols // 2, slot_rows) if last else (slot_rows, cols)
    sum_specs = [pl.BlockSpec((1, slot_rows, cols), lambda j, w: (j, 0, 0))] if last else []
    grid_spec = pltpu.PrefetchScalarGridSpec(
        num_scalar_prefetch=1,
        grid=(2,),
        in_specs=[
            pl.BlockSpec((1, depth, cols), lambda j, w: (j, 0, 0)),
            pl.BlockSpec((peers, zs, deltas.shape[2]), lambda j, w: (0, j, 0)),
            pl.BlockSpec((1, 1, br * learners), lambda j, w: (j, 0, 0)),
        ]
        + [pl.BlockSpec((peers, rows // 2, quarter), lambda j, w: (0, j, 0))] * len(toks)
        + sum_specs,
        out_specs=pl.BlockSpec((1, *shape), lambda j, w: (j, 0, 0)),
        scratch_shapes=[pltpu.VMEM((br * learners, cols), BF)],
    )
    return pl.pallas_call(
        functools.partial(gate_kernel, br, last),
        grid_spec=grid_spec,
        out_shape=jax.ShapeDtypeStruct((2, *shape), BF if last else F32),
        compiler_params=PARAMS,
        cost_estimate=pl.CostEstimate(
            flops=len(toks) * depth * cols * (slot_rows + br * learners),
            bytes_accessed=10 * 1024 * 1024,
            transcendentals=2 * slot_rows * cols,
        ),
    )(where, gate_up, deltas, targets, *toks, *([sums] if last else []))


def down_kernel(br, w_ref, d_ref, t_ref, out_ref, cat_ref):
    peers, zs, _ = d_ref.shape
    depth, cols = w_ref.shape[1:]
    learners = peers * zs
    for r in range(br):
        cat_ref[r * learners : (r + 1) * learners, :] = d_ref[
            :, :, r * cols : (r + 1) * cols
        ].reshape(learners, cols)
    row_ids = lax.broadcasted_iota(jnp.int32, (depth, br * learners), 0)
    spread = jnp.where(row_ids == t_ref[0], 1.0, 0.0).astype(BF)
    update = jnp.dot(spread, cat_ref[...], preferred_element_type=F32)
    out_ref[0] = (w_ref[0].astype(F32) + update).astype(BF)


def fresh_down(down, deltas, targets, br):
    _, depth, cols = down.shape
    peers, zs = deltas.shape[0], deltas.shape[1] // 2
    learners = peers * zs
    return pl.pallas_call(
        functools.partial(down_kernel, br),
        grid=(2,),
        in_specs=[
            pl.BlockSpec((1, depth, cols), lambda j: (j, 0, 0)),
            pl.BlockSpec((peers, zs, deltas.shape[2]), lambda j: (0, j, 0)),
            pl.BlockSpec((1, 1, br * learners), lambda j: (j, 0, 0)),
        ],
        out_specs=pl.BlockSpec((1, depth, cols), lambda j: (j, 0, 0)),
        scratch_shapes=[pltpu.VMEM((br * learners, cols), BF)],
        out_shape=jax.ShapeDtypeStruct((2, depth, cols), BF),
        compiler_params=PARAMS,
        cost_estimate=pl.CostEstimate(
            flops=4 * depth * cols * br * learners,
            bytes_accessed=5 * 1024 * 1024,
            transcendentals=0,
        ),
    )(down, deltas, targets)


def out_kernel(peers, h0_ref, h1_ref, w_ref, out_ref):
    parts, hd, slot_rows = h0_ref.shape
    cols = w_ref.shape[2]
    for j, h_ref in enumerate((h0_ref, h1_ref)):
        acc = None
        for p in range(parts):
            term = lax.dot_general(
                h_ref[p],
                w_ref[j, p * hd : (p + 1) * hd, :],
                (((0,), (0,)), ((), ())),
                preferred_element_type=F32,
            )
            acc = term if acc is None else acc + term
        out_ref[:, j] = acc.astype(BF).reshape(peers, slot_rows // peers, cols)


def expert_out(h0, h1, down, peers):
    parts, hd, slot_rows = h0.shape
    cols = down.shape[2]
    return pl.pallas_call(
        functools.partial(out_kernel, peers),
        out_shape=jax.ShapeDtypeStruct((peers, 2, slot_rows // peers, cols), BF),
        compiler_params=PARAMS,
        cost_estimate=pl.CostEstimate(
            flops=4 * slot_rows * cols * parts * hd,
            bytes_accessed=5 * 1024 * 1024,
            transcendentals=0,
        ),
    )(h0, h1, down)


def mix_kernel(ret_ref, code_ref, gate_ref, target_ref, out_ref):
    peers, _, steps, part, width = ret_ref.shape
    _, count, top = code_ref.shape
    zs, rows2, _ = out_ref.shape
    rows = rows2 // steps
    slots = peers * 2 * part
    own = lax.broadcasted_iota(jnp.int32, (count, slots), 1) % part // CAP
    held = lax.broadcasted_iota(jnp.int32, (count, slots), 0) // rows
    same = own == held
    target = target_ref[...]
    for s in range(steps):
        weight = jnp.zeros((count, slots), F32)
        for k in range(top):
            hit = code_ref[s, :, k : k + 1] == target
            weight = jnp.where(hit, gate_ref[s, :, k : k + 1], weight)
        weight = jnp.where(same, weight, 0.0)
        back = ret_ref[:, :, s].reshape(slots, width)
        high = weight.astype(BF)
        rest = weight - high.astype(F32)
        mid = rest.astype(BF)
        low = (rest - mid.astype(F32)).astype(BF)
        total = (
            jnp.dot(high, back, preferred_element_type=F32)
            + jnp.dot(mid, back, preferred_element_type=F32)
            + jnp.dot(low, back, preferred_element_type=F32)
        )
        out_ref[:, s * rows : (s + 1) * rows, :] = total.astype(BF).reshape(zs, rows, width)


def mix_rows(back, codes, gates, target_row, zs, rows2):
    width = back.shape[-1]
    return pl.pallas_call(
        mix_kernel,
        out_shape=jax.ShapeDtypeStruct((zs, rows2, width), BF),
        compiler_params=PARAMS,
        cost_estimate=pl.CostEstimate(
            flops=12 * codes.shape[1] * target_row.shape[1] * width,
            bytes_accessed=2 * 1024 * 1024,
            transcendentals=0,
        ),
    )(back, codes, gates, target_row)


def on_device(
    tokens,
    route_ids,
    gate_vals,
    replica_choice,
    placement,
    gate_up,
    down_proj,
    changed_expert,
    changed_block,
    delta_gate_up,
    delta_down,
):
    nx, nz, nc, nd = (lax.axis_size(a) for a in ("x", "z", "c", "dp"))
    peers = nx * nc
    steps, rows, quarter = tokens.shape
    top = route_ids.shape[2]
    changed, br, gate_cols = delta_gate_up.shape[1:]
    br2, down_cols = delta_down.shape[2:]
    z = lax.axis_index("z")
    p = lax.axis_index("dp")

    flat_deltas = jnp.concatenate(
        [delta_gate_up.reshape(changed, -1), delta_down.reshape(changed, -1)], axis=1
    )
    deltas = lax.all_gather(flat_deltas, "z", axis=0, tiled=True)

    codes = slot_codes(route_ids, replica_choice[:, 0], placement)
    high = lax.reduce_precision(gate_vals, 8, 7)
    mid = lax.reduce_precision(gate_vals - high, 8, 7)
    low = gate_vals - high - mid
    meta = jnp.concatenate([codes.astype(F32), high, mid, low], axis=2).reshape(
        steps * rows, 4 * top
    )
    names = jnp.stack([changed_expert[0], changed_block[0]], axis=1).astype(F32)
    meta = jnp.concatenate([meta, names], axis=1)
    meta = jnp.pad(meta, ((0, 0), (0, META - meta.shape[1]))).astype(BF)
    packet = jnp.concatenate([tokens.reshape(steps * rows, quarter), meta], axis=1)
    packets = lax.all_gather(packet, "z", axis=0, tiled=False)

    metas = packets[:, :, quarter:].astype(F32)
    gathered = metas.reshape(nz, steps, rows, META).transpose(1, 0, 2, 3)
    gathered = gathered.reshape(steps, nz * rows, META)
    codes_all = gathered[:, :, :top]
    gates_all = (
        gathered[:, :, top : 2 * top]
        + gathered[:, :, 2 * top : 3 * top]
        + gathered[:, :, 3 * top : 4 * top]
    )
    codes_t = codes_all.transpose(0, 2, 1)
    names_expert = metas[:, :, 4 * top]
    names_block = metas[:, :, 4 * top + 1]

    devs = (
        jnp.arange(nx, dtype=jnp.int32)[:, None] * nz + z
    ) * nc + jnp.arange(nc, dtype=jnp.int32)[None, :]
    devs = devs.reshape(peers)
    slot_ids = devs[:, None] * 2 + jnp.arange(2, dtype=jnp.int32)[None, :]
    target = slot_ids[:, :, None, None] * CAP + jnp.arange(CAP, dtype=jnp.int32)
    target = jnp.broadcast_to(target, (peers, 2, nz, CAP)).reshape(-1)
    target = (target - nx * nz * nc * CAP).astype(F32)

    held = lax.dynamic_index_in_dim(
        placement.reshape(nx, nz, nc, 2), z, axis=1, keepdims=False
    ).reshape(peers, 2)
    held = held.astype(F32)
    match = held[:, :, None, None] == names_expert[None, None]
    labels = jnp.sum(jnp.where(match, names_block + 1.0, 0.0), axis=3)
    labels = labels.reshape(peers, 1, 2 * nz).astype(BF)
    labels = jnp.pad(labels, ((0, 0), (0, 15), (0, quarter - 2 * nz)))
    z_ids = jnp.arange(nz, dtype=jnp.int32)
    chosen = (
        match[:, :, None, :, :] & (z_ids[:, None] == z_ids[None, :])[None, None, :, :, None]
    )
    chosen = chosen.astype(BF).reshape(peers * 2 * nz, nz * changed)

    count_rows = 2 * steps * nz * CAP
    picked = pick_rows(
        packets, codes_t, target[:, None], labels, quarter, peers, count_rows
    )
    got = lax.all_to_all(picked, XC, split_axis=0, concat_axis=0, tiled=True)
    own = got[:, :count_rows]
    toks = [own] + [
        lax.ppermute(own, "dp", [(i, (i + n) % nd) for i in range(nd)]) for n in range(1, nd)
    ]
    block_of = got[:, count_rows, : 2 * nz].astype(F32).astype(jnp.int32) - 1
    block_of = block_of.reshape(peers, 2, nz).transpose(1, 0, 2).reshape(2, 1, peers * nz)
    gate_targets = (block_of * br + jnp.arange(br, dtype=jnp.int32)[None, :, None]).reshape(
        2, 1, -1
    )
    down_targets = (block_of * br2 + jnp.arange(br2, dtype=jnp.int32)[None, :, None]).reshape(
        2, 1, -1
    )

    cut = br * gate_cols
    near = [0] + [n for n in range(1, nd) if n in (1, nd - 1)]
    far = [n for n in range(1, nd) if n not in near]
    where_near = jnp.stack([(p - n) % nd for n in near]).astype(jnp.int32)
    where_far = jnp.stack([(p - n) % nd for n in far]).astype(jnp.int32)
    send_gate = jnp.dot(chosen, deltas[:, :cut], preferred_element_type=F32).astype(BF)
    send_gate, *_ = lax.optimization_barrier((send_gate, toks[1], toks[-1]))
    got_gate = lax.all_to_all(
        send_gate.reshape(peers, 2 * nz, cut), XC, split_axis=0, concat_axis=0, tiled=True
    )
    send_down = jnp.dot(chosen, deltas[:, cut:], preferred_element_type=F32).astype(BF)
    sums = gate_hidden(
        where_near, gate_up[0], got_gate, gate_targets, [toks[n] for n in near], br
    )
    send_down, sums = lax.optimization_barrier((send_down, sums))
    got_down = lax.all_to_all(
        send_down.reshape(peers, 2 * nz, br2 * down_cols),
        XC,
        split_axis=0,
        concat_axis=0,
        tiled=True,
    )
    hidden = gate_hidden(
        where_far,
        gate_up[0],
        got_gate,
        gate_targets,
        [toks[n] for n in far],
        br,
        sums,
    )
    down = fresh_down(down_proj[0], got_down, down_targets, br2)
    h0 = lax.all_gather(hidden[0], "dp", axis=0, tiled=False)
    h1 = lax.all_gather(hidden[1], "dp", axis=0, tiled=False)
    out = expert_out(h0, h1, down, peers).reshape(peers, count_rows, down_cols)

    back = lax.all_to_all(out, XC, split_axis=0, concat_axis=0, tiled=True)
    back = back.reshape(peers, 2, steps, nz * CAP, down_cols)
    partial = mix_rows(back, codes_all, gates_all, target[None, :], nz, steps * rows)
    final = lax.all_to_all(partial, "z", split_axis=0, concat_axis=0, tiled=True)
    total = jnp.sum(final.astype(F32), axis=0).astype(BF)
    return total.reshape(steps, rows, down_cols)


def solution(mesh):
    ep, nd = mesh.devices.shape
    cube = Mesh(mesh.devices.reshape(NX, ep // (NX * NC), NC, nd), EP + ("dp",))
    return jax.shard_map(
        on_device,
        mesh=cube,
        in_specs=(
            P(None, EP, "dp"),
            P(None, EP, None),
            P(None, EP, None),
            P(None, EP, None),
            P(),
            P(EP, None, None, "dp"),
            P(EP, None, None, "dp"),
            P(EP, None),
            P(EP, None),
            P(EP, None, None, "dp"),
            P(EP, None, None, "dp"),
        ),
        out_specs=P(None, EP, "dp"),
        check_vma=False,
    )
```

```python
import functools

import jax
import jax.numpy as jnp
from jax import lax
from jax.experimental import pallas as pl
from jax.experimental.pallas import tpu as pltpu
from jax.sharding import Mesh, PartitionSpec as P

NX = 4
NC = 2
EP = ("x", "z", "c")
XC = ("x", "c")
CAP = 2
META = 128
BF = jnp.bfloat16
F32 = jnp.float32
PARAMS = pltpu.CompilerParams(vmem_limit_bytes=40 * 1024 * 1024)
WIDE = pltpu.CompilerParams(vmem_limit_bytes=60 * 1024 * 1024)


def slot_codes(route, choice, placement):
    steps, rows, top = route.shape
    experts = choice.shape[1]
    devices = placement.shape[0]
    expert_ids = jnp.arange(experts, dtype=jnp.int32)
    device_ids = jnp.arange(devices, dtype=jnp.int32)
    host = jnp.sum(
        jnp.where(placement[:, :, None] == expert_ids, device_ids[:, None, None], 0), axis=0
    )
    table = jnp.where(choice == 1, host[1] * 2 + 1, host[0] * 2)
    flat = route.reshape(steps, rows * top)
    slot = jnp.sum(
        jnp.where(flat[:, :, None] == expert_ids, table[:, None, :], 0), axis=2
    )
    order = jnp.arange(rows * top, dtype=jnp.int32)
    position = jnp.sum(
        ((flat[:, :, None] == flat[:, None, :]) & (order[None, :] < order[:, None])).astype(
            jnp.int32
        ),
        axis=2,
    )
    return (slot * CAP + position - devices * CAP).reshape(steps, rows, top)


def pick_kernel(tok_ref, code_ref, target_ref, label_ref, out_ref):
    zs, rows2, _ = tok_ref.shape
    peers, _, width = out_ref.shape
    steps, top, count = code_ref.shape
    rows = rows2 // steps
    slots = target_ref.shape[0]
    part = slots // (peers * 2)
    own = lax.broadcasted_iota(jnp.int32, (slots, count), 0) % part // CAP
    held = lax.broadcasted_iota(jnp.int32, (slots, count), 1) // rows
    same = own == held
    target = target_ref[...]
    for s in range(steps):
        hit = code_ref[s, 0:1, :] == target
        for k in range(1, top):
            hit = hit | (code_ref[s, k : k + 1, :] == target)
        pick = jnp.where(hit & same, 1.0, 0.0).astype(BF)
        toks = tok_ref[:, s * rows : (s + 1) * rows, :width].reshape(count, width)
        got = jnp.dot(pick, toks, preferred_element_type=F32).astype(BF)
        got = got.reshape(peers, 2, part, width)
        for j in range(2):
            start = (j * steps + s) * part
            out_ref[:, start : start + part, :] = got[:, j]
    out_ref[:, 2 * steps * part :, :] = label_ref[...]


def pick_rows(packets, codes_t, target_col, labels, width, peers, rows):
    return pl.pallas_call(
        pick_kernel,
        out_shape=jax.ShapeDtypeStruct((peers, rows + 16, width), BF),
        compiler_params=PARAMS,
        cost_estimate=pl.CostEstimate(
            flops=4 * codes_t.shape[2] * target_col.shape[0] * width,
            bytes_accessed=4 * 1024 * 1024,
            transcendentals=0,
        ),
    )(packets, codes_t, target_col, labels)


def gate_kernel(br, last, where_ref, w_ref, d_ref, t_ref, *refs):
    tok_refs, out_ref, cat_ref = refs[:-2], refs[-2], refs[-1]
    if last:
        tok_refs, sum_ref = tok_refs[:-1], tok_refs[-1]
    peers, zs, _ = d_ref.shape
    depth, cols = w_ref.shape[1:]
    learners = peers * zs
    quarter = tok_refs[0].shape[2]
    parts = len(tok_refs)
    for r in range(br):
        cat_ref[r * learners : (r + 1) * learners, :] = d_ref[
            :, :, r * cols : (r + 1) * cols
        ].reshape(learners, cols)
    chunk = min(256, quarter)
    row_ids = lax.broadcasted_iota(jnp.int32, (chunk, br * learners), 0)
    tgt = t_ref[0]
    acc = sum_ref[0] if last else None
    for n in range(parts):
        q = where_ref[n]
        for c in range(quarter // chunk):
            base = pl.multiple_of(q * quarter + c * chunk, chunk)
            spread = jnp.where(row_ids == tgt - base, 1.0, 0.0).astype(BF)
            update = jnp.dot(spread, cat_ref[...], preferred_element_type=F32)
            fresh = (w_ref[0, pl.ds(base, chunk), :].astype(F32) + update).astype(BF)
            toks = tok_refs[n][:, :, c * chunk : (c + 1) * chunk].reshape(-1, chunk)
            term = jnp.dot(toks, fresh, preferred_element_type=F32)
            acc = term if acc is None else acc + term
    if not last:
        out_ref[0] = acc
        return
    half = cols // 2
    up = pltpu.roll(acc, half, 1)
    act = acc / (1.0 + jnp.exp(-acc)) * up
    out_ref[0] = act.T[:half].astype(BF)


def gate_hidden(where, gate_up, deltas, targets, toks, br, sums=None):
    last = sums is not None
    _, depth, cols = gate_up.shape
    peers, rows, quarter = toks[0].shape
    zs = deltas.shape[1] // 2
    slot_rows = peers * rows // 2
    learners = peers * zs
    shape = (cols // 2, slot_rows) if last else (slot_rows, cols)
    sum_specs = [pl.BlockSpec((1, slot_rows, cols), lambda j, w: (j, 0, 0))] if last else []
    grid_spec = pltpu.PrefetchScalarGridSpec(
        num_scalar_prefetch=1,
        grid=(2,),
        in_specs=[
            pl.BlockSpec((1, depth, cols), lambda j, w: (j, 0, 0)),
            pl.BlockSpec((peers, zs, deltas.shape[2]), lambda j, w: (0, j, 0)),
            pl.BlockSpec((1, 1, br * learners), lambda j, w: (j, 0, 0)),
        ]
        + [pl.BlockSpec((peers, rows // 2, quarter), lambda j, w: (0, j, 0))] * len(toks)
        + sum_specs,
        out_specs=pl.BlockSpec((1, *shape), lambda j, w: (j, 0, 0)),
        scratch_shapes=[pltpu.VMEM((br * learners, cols), BF)],
    )
    return pl.pallas_call(
        functools.partial(gate_kernel, br, last),
        grid_spec=grid_spec,
        out_shape=jax.ShapeDtypeStruct((2, *shape), BF if last else F32),
        compiler_params=WIDE,
        cost_estimate=pl.CostEstimate(
            flops=len(toks) * depth * cols * (slot_rows + br * learners),
            bytes_accessed=10 * 1024 * 1024,
            transcendentals=2 * slot_rows * cols,
        ),
    )(where, gate_up, deltas, targets, *toks, *([sums] if last else []))


def down_kernel(br, w_ref, d_ref, t_ref, out_ref, cat_ref):
    peers, zs, _ = d_ref.shape
    depth, cols = w_ref.shape[1:]
    learners = peers * zs
    for r in range(br):
        cat_ref[r * learners : (r + 1) * learners, :] = d_ref[
            :, :, r * cols : (r + 1) * cols
        ].reshape(learners, cols)
    row_ids = lax.broadcasted_iota(jnp.int32, (depth, br * learners), 0)
    spread = jnp.where(row_ids == t_ref[0], 1.0, 0.0).astype(BF)
    update = jnp.dot(spread, cat_ref[...], preferred_element_type=F32)
    out_ref[0] = (w_ref[0].astype(F32) + update).astype(BF)


def fresh_down(down, deltas, targets, br):
    _, depth, cols = down.shape
    peers, zs = deltas.shape[0], deltas.shape[1] // 2
    learners = peers * zs
    return pl.pallas_call(
        functools.partial(down_kernel, br),
        grid=(2,),
        in_specs=[
            pl.BlockSpec((1, depth, cols), lambda j: (j, 0, 0)),
            pl.BlockSpec((peers, zs, deltas.shape[2]), lambda j: (0, j, 0)),
            pl.BlockSpec((1, 1, br * learners), lambda j: (j, 0, 0)),
        ],
        out_specs=pl.BlockSpec((1, depth, cols), lambda j: (j, 0, 0)),
        scratch_shapes=[pltpu.VMEM((br * learners, cols), BF)],
        out_shape=jax.ShapeDtypeStruct((2, depth, cols), BF),
        compiler_params=PARAMS,
        cost_estimate=pl.CostEstimate(
            flops=4 * depth * cols * br * learners,
            bytes_accessed=5 * 1024 * 1024,
            transcendentals=0,
        ),
    )(down, deltas, targets)


def out_kernel(peers, h0_ref, h1_ref, w_ref, out_ref):
    parts, hd, slot_rows = h0_ref.shape
    cols = w_ref.shape[2]
    for j, h_ref in enumerate((h0_ref, h1_ref)):
        acc = None
        for p in range(parts):
            term = lax.dot_general(
                h_ref[p],
                w_ref[j, p * hd : (p + 1) * hd, :],
                (((0,), (0,)), ((), ())),
                preferred_element_type=F32,
            )
            acc = term if acc is None else acc + term
        out_ref[:, j] = acc.astype(BF).reshape(peers, slot_rows // peers, cols)


def expert_out(h0, h1, down, peers):
    parts, hd, slot_rows = h0.shape
    cols = down.shape[2]
    return pl.pallas_call(
        functools.partial(out_kernel, peers),
        out_shape=jax.ShapeDtypeStruct((peers, 2, slot_rows // peers, cols), BF),
        compiler_params=PARAMS,
        cost_estimate=pl.CostEstimate(
            flops=4 * slot_rows * cols * parts * hd,
            bytes_accessed=5 * 1024 * 1024,
            transcendentals=0,
        ),
    )(h0, h1, down)


def mix_kernel(ret_ref, code_ref, gate_ref, target_ref, out_ref):
    peers, _, steps, part, width = ret_ref.shape
    _, count, top = code_ref.shape
    zs, rows2, _ = out_ref.shape
    rows = rows2 // steps
    slots = peers * 2 * part
    own = lax.broadcasted_iota(jnp.int32, (count, slots), 1) % part // CAP
    held = lax.broadcasted_iota(jnp.int32, (count, slots), 0) // rows
    same = own == held
    target = target_ref[...]
    for s in range(steps):
        weight = jnp.zeros((count, slots), F32)
        for k in range(top):
            hit = code_ref[s, :, k : k + 1] == target
            weight = jnp.where(hit, gate_ref[s, :, k : k + 1], weight)
        weight = jnp.where(same, weight, 0.0)
        back = ret_ref[:, :, s].reshape(slots, width)
        high = weight.astype(BF)
        rest = weight - high.astype(F32)
        mid = rest.astype(BF)
        low = (rest - mid.astype(F32)).astype(BF)
        total = (
            jnp.dot(high, back, preferred_element_type=F32)
            + jnp.dot(mid, back, preferred_element_type=F32)
            + jnp.dot(low, back, preferred_element_type=F32)
        )
        out_ref[:, s * rows : (s + 1) * rows, :] = total.astype(BF).reshape(zs, rows, width)


def mix_rows(back, codes, gates, target_row, zs, rows2):
    width = back.shape[-1]
    return pl.pallas_call(
        mix_kernel,
        out_shape=jax.ShapeDtypeStruct((zs, rows2, width), BF),
        compiler_params=PARAMS,
        cost_estimate=pl.CostEstimate(
            flops=12 * codes.shape[1] * target_row.shape[1] * width,
            bytes_accessed=2 * 1024 * 1024,
            transcendentals=0,
        ),
    )(back, codes, gates, target_row)


def on_device(
    tokens,
    route_ids,
    gate_vals,
    replica_choice,
    placement,
    gate_up,
    down_proj,
    changed_expert,
    changed_block,
    delta_gate_up,
    delta_down,
):
    nx, nz, nc, nd = (lax.axis_size(a) for a in ("x", "z", "c", "dp"))
    peers = nx * nc
    steps, rows, quarter = tokens.shape
    top = route_ids.shape[2]
    changed, br, gate_cols = delta_gate_up.shape[1:]
    br2, down_cols = delta_down.shape[2:]
    z = lax.axis_index("z")
    p = lax.axis_index("dp")

    flat_deltas = jnp.concatenate(
        [delta_gate_up.reshape(changed, -1), delta_down.reshape(changed, -1)], axis=1
    )
    deltas = lax.all_gather(flat_deltas, "z", axis=0, tiled=True)

    codes = slot_codes(route_ids, replica_choice[:, 0], placement)
    high = lax.reduce_precision(gate_vals, 8, 7)
    mid = lax.reduce_precision(gate_vals - high, 8, 7)
    low = gate_vals - high - mid
    meta = jnp.concatenate([codes.astype(F32), high, mid, low], axis=2).reshape(
        steps * rows, 4 * top
    )
    names = jnp.stack([changed_expert[0], changed_block[0]], axis=1).astype(F32)
    meta = jnp.concatenate([meta, names], axis=1)
    meta = jnp.pad(meta, ((0, 0), (0, META - meta.shape[1]))).astype(BF)
    packet = jnp.concatenate([tokens.reshape(steps * rows, quarter), meta], axis=1)
    packets = lax.all_gather(packet, "z", axis=0, tiled=False)

    metas = packets[:, :, quarter:].astype(F32)
    gathered = metas.reshape(nz, steps, rows, META).transpose(1, 0, 2, 3)
    gathered = gathered.reshape(steps, nz * rows, META)
    codes_all = gathered[:, :, :top]
    gates_all = (
        gathered[:, :, top : 2 * top]
        + gathered[:, :, 2 * top : 3 * top]
        + gathered[:, :, 3 * top : 4 * top]
    )
    codes_t = codes_all.transpose(0, 2, 1)
    names_expert = metas[:, :, 4 * top]
    names_block = metas[:, :, 4 * top + 1]

    devs = (
        jnp.arange(nx, dtype=jnp.int32)[:, None] * nz + z
    ) * nc + jnp.arange(nc, dtype=jnp.int32)[None, :]
    devs = devs.reshape(peers)
    slot_ids = devs[:, None] * 2 + jnp.arange(2, dtype=jnp.int32)[None, :]
    target = slot_ids[:, :, None, None] * CAP + jnp.arange(CAP, dtype=jnp.int32)
    target = jnp.broadcast_to(target, (peers, 2, nz, CAP)).reshape(-1)
    target = (target - nx * nz * nc * CAP).astype(F32)

    held = lax.dynamic_index_in_dim(
        placement.reshape(nx, nz, nc, 2), z, axis=1, keepdims=False
    ).reshape(peers, 2)
    held = held.astype(F32)
    match = held[:, :, None, None] == names_expert[None, None]
    labels = jnp.sum(jnp.where(match, names_block + 1.0, 0.0), axis=3)
    labels = labels.reshape(peers, 1, 2 * nz).astype(BF)
    labels = jnp.pad(labels, ((0, 0), (0, 15), (0, quarter - 2 * nz)))
    z_ids = jnp.arange(nz, dtype=jnp.int32)
    chosen = (
        match[:, :, None, :, :] & (z_ids[:, None] == z_ids[None, :])[None, None, :, :, None]
    )
    chosen = chosen.astype(BF).reshape(peers * 2 * nz, nz * changed)

    count_rows = 2 * steps * nz * CAP
    picked = pick_rows(
        packets, codes_t, target[:, None], labels, quarter, peers, count_rows
    )
    got = lax.all_to_all(picked, XC, split_axis=0, concat_axis=0, tiled=True)
    own = got[:, :count_rows]
    toks = [own] + [
        lax.ppermute(own, "dp", [(i, (i + n) % nd) for i in range(nd)]) for n in range(1, nd)
    ]
    block_of = got[:, count_rows, : 2 * nz].astype(F32).astype(jnp.int32) - 1
    block_of = block_of.reshape(peers, 2, nz).transpose(1, 0, 2).reshape(2, 1, peers * nz)
    gate_targets = (block_of * br + jnp.arange(br, dtype=jnp.int32)[None, :, None]).reshape(
        2, 1, -1
    )
    down_targets = (block_of * br2 + jnp.arange(br2, dtype=jnp.int32)[None, :, None]).reshape(
        2, 1, -1
    )

    cut = br * gate_cols
    near = [0] + [n for n in range(1, nd) if n in (1, nd - 1)]
    far = [n for n in range(1, nd) if n not in near]
    where_near = jnp.stack([(p - n) % nd for n in near]).astype(jnp.int32)
    where_far = jnp.stack([(p - n) % nd for n in far]).astype(jnp.int32)
    send_gate = jnp.dot(chosen, deltas[:, :cut], preferred_element_type=F32).astype(BF)
    send_gate, *_ = lax.optimization_barrier((send_gate, toks[1], toks[-1]))
    got_gate = lax.all_to_all(
        send_gate.reshape(peers, 2 * nz, cut), XC, split_axis=0, concat_axis=0, tiled=True
    )
    send_down = jnp.dot(chosen, deltas[:, cut:], preferred_element_type=F32).astype(BF)
    sums = gate_hidden(
        where_near, gate_up[0], got_gate, gate_targets, [toks[n] for n in near], br
    )
    send_down, sums = lax.optimization_barrier((send_down, sums))
    got_down = lax.all_to_all(
        send_down.reshape(peers, 2 * nz, br2 * down_cols),
        XC,
        split_axis=0,
        concat_axis=0,
        tiled=True,
    )
    hidden = gate_hidden(
        where_far,
        gate_up[0],
        got_gate,
        gate_targets,
        [toks[n] for n in far],
        br,
        sums,
    )
    down = fresh_down(down_proj[0], got_down, down_targets, br2)
    h0 = lax.all_gather(hidden[0], "dp", axis=0, tiled=False)
    h1 = lax.all_gather(hidden[1], "dp", axis=0, tiled=False)
    out = expert_out(h0, h1, down, peers).reshape(peers, count_rows, down_cols)

    back = lax.all_to_all(out, XC, split_axis=0, concat_axis=0, tiled=True)
    back = back.reshape(peers, 2, steps, nz * CAP, down_cols)
    partial = mix_rows(back, codes_all, gates_all, target[None, :], nz, steps * rows)
    final = lax.all_to_all(partial, "z", split_axis=0, concat_axis=0, tiled=True)
    total = jnp.sum(final.astype(F32), axis=0).astype(BF)
    return total.reshape(steps, rows, down_cols)


def solution(mesh):
    ep, nd = mesh.devices.shape
    cube = Mesh(mesh.devices.reshape(NX, ep // (NX * NC), NC, nd), EP + ("dp",))
    return jax.shard_map(
        on_device,
        mesh=cube,
        in_specs=(
            P(None, EP, "dp"),
            P(None, EP, None),
            P(None, EP, None),
            P(None, EP, None),
            P(),
            P(EP, None, None, "dp"),
            P(EP, None, None, "dp"),
            P(EP, None),
            P(EP, None),
            P(EP, None, None, "dp"),
            P(EP, None, None, "dp"),
        ),
        out_specs=P(None, EP, "dp"),
        check_vma=False,
    )
```
